32 devices in a mesh: px: 4 (over x, core), py: 8 (over z, y).
Axes of the slice: x: 2, y: 2, z: 4, core: 2. Of those that a mesh axis runs over, the one named last changes fastest.
Arguments:
- right_side: float32 [4, 8, 16, 8, 128], P('px', 'py'), may hold values from -6 to 6
- live_blocks: int32 [4, 8], P('px', 'py'), may hold values from 8 to 16, as said below
- diag_fine: float32 [4, 8, 16, 128, 128], P('px', 'py')
- couple_fine: float32 [4, 8, 16, 4, 128, 128], P('px', 'py'), may hold values from -0.125 to 0.125
- links_fine: int32 [4, 8, 16, 4], P('px', 'py'), may hold values from 0 to 31
- send_fine: int32 [4, 8, 4], P('px', 'py'), may hold values from 0 to 7
- prolong_fine: float32 [4, 8, 16, 128, 128], P('px', 'py'), may hold values from -0.25 to 0.25
- owner_fine: int32 [4, 8, 16], P('px', 'py'), may hold values from 0 to 3
- diag_mid: float32 [4, 8, 4, 128, 128], P('px', 'py')
- couple_mid: float32 [4, 8, 4, 4, 128, 128], P('px', 'py'), may hold values from -0.125 to 0.125
- links_mid: int32 [4, 8, 4, 4], P('px', 'py'), may hold values from 0 to 7
- send_mid: int32 [4, 8, 1], P('px', 'py'), may hold values from 0 to 3
- prolong_mid: float32 [4, 8, 4, 128, 128], P('px', 'py'), may hold values from -0.375 to 0.375
- owner_mid: int32 [4, 8, 4], P('px', 'py'), may hold values from 0 to 3
- diag_row: float32 [4, 4, 128, 128], P('px')
- couple_row: float32 [4, 4, 4, 128, 128], P('px'), may hold values from -0.125 to 0.125
- links_row: int32 [4, 4, 4], P('px'), may hold values from 0 to 5
- send_row: int32 [4, 1], P('px'), may hold values from 0 to 3
- prolong_row: float32 [4, 4, 128, 128], P('px'), may hold values from -0.375 to 0.375
- owner_row: int32 [4, 4], P('px'), may hold values from 0 to 3
- coarse_inverse: float32 [512, 512], replicated, may hold values from -0.25 to 0.25
- cheb_low: float32 [3], replicated, may hold values from 0.3 to 0.8
- cheb_high: float32 [3], replicated, may hold values from 6.5 to 9
Outputs:
- solution: float32 [4, 8, 16, 8, 128], P('px', 'py')
- residual: float32 [4, 8, 16, 8, 128], P('px', 'py')
The draws below stay inside these ranges and needn't reach their ends.
Inputs may be any that keep to these rules, and one draw needn't show every extreme that they name: `live_blocks`: each partition's live fine blocks are its first ones, the rest of its 16 blocks are padding.
All inputs are finite; a program needn't handle non-finite values.
Results may differ from the reference program's by a relative error of at most 0.000092.
Values sent between devices are 32-bit elements; how exact they have to be, the bound alone decides.
A program may use at most 64 MiB of HBM per device.

```python
import math
import jax
import jax.numpy as jnp
from jax import lax

F = 16
NODE = 128
R = 8
K = 4
H0 = 4
H1 = 1
H2 = 1
G2 = 4
G3 = 4
LEVELS = 4
MID = 4
PROWS = 4
PCOLS = 8


def block_draw(key, block_shape):
    node_count = block_shape[-1]
    main_key, side_key = jax.random.split(key)
    level_gain = jax.random.uniform(main_key, block_shape[:-1], jnp.float32, 3.0, 5.0)
    off_diag = jax.random.normal(side_key, block_shape, jnp.float32) * 0.5
    identity = jnp.eye(node_count, dtype=jnp.float32)
    return level_gain[..., None] * identity + off_diag / node_count ** 0.5


def draw_diag_fine(key, part):
    return block_draw(jax.random.fold_in(key, 11), (PROWS, PCOLS, F, NODE, NODE))


def draw_diag_mid(key, part):
    return block_draw(jax.random.fold_in(key, 12), (PROWS, PCOLS, MID, NODE, NODE))


def draw_diag_row(key, part):
    return block_draw(jax.random.fold_in(key, 13), (PROWS, G2, NODE, NODE))


def draw_live_blocks(key, part):
    count_key, spot_key = jax.random.split(jax.random.fold_in(key, 21))
    total = PROWS * PCOLS
    counts = jax.random.randint(count_key, (total,), F // 2, F + 1, dtype=jnp.int32)
    full_spot = jax.random.randint(spot_key, (), 0, total, dtype=jnp.int32)
    positions = jnp.arange(total, dtype=jnp.int32)
    counts = jnp.where(positions == full_spot, F, counts)
    counts = jnp.where(positions == (full_spot + 1) % total, F // 2, counts)
    return counts.reshape(PROWS, PCOLS).astype(jnp.int32)


def with_ends(entries, own_key, least, high):
    longest = entries.shape.index(max(entries.shape))
    spots = []
    for shift in (0, 1):
        where = [jax.random.randint(jax.random.fold_in(own_key, axis), (), 0, length) for axis, length in enumerate(entries.shape)]
        where[longest] = (where[longest] + shift) % entries.shape[longest]
        spots.append(tuple(where))
    return entries.at[spots[0]].set(least).at[spots[1]].set(high)


def shard_levels(rng, shape, cuts, least, largest):
    loudness, own = 1.0, jax.random.fold_in(rng, 6)
    for position, blocks in cuts:
        steps = jnp.exp(jax.random.uniform(jax.random.fold_in(own, position), (blocks,), jnp.float32, least / len(cuts), largest / len(cuts)))
        loudness = loudness * jnp.repeat(steps, shape[position] // blocks).reshape([-1 if axis == position else 1 for axis in range(len(shape))])
    return loudness


def centred(key, shape, scale, most, cuts=(), kind=jnp.bfloat16):
    level = shard_levels(key, shape, cuts, -0.22, 0.18) if cuts else 1.0
    entries = jax.random.normal(key, shape, jnp.float32) * scale * level
    return jnp.minimum(jnp.maximum(entries, -most), most).astype(kind)


def setup_inputs(seed: int = 0) -> dict:
    splits = jax.random.split(jax.random.key(seed), 24)
    return {
        "right_side": centred(splits[0], (PROWS, PCOLS, F, R, NODE), 1.0, 6.0, ((0, 4), (1, 8)), jnp.float32),
        "live_blocks": draw_live_blocks(jax.random.fold_in(splits[23], 71), 0),
        "diag_fine": draw_diag_fine(jax.random.fold_in(splits[23], 71), 0),
        "couple_fine": centred(splits[3], (PROWS, PCOLS, F, K, NODE, NODE), (16 * NODE) ** -0.5, 0.125, ((0, 4), (1, 8)), jnp.float32),
        "links_fine": with_ends(jax.random.randint(splits[4], (PROWS, PCOLS, F, K), 0, F + 4 * H0), jax.random.fold_in(splits[4], 1), 0, (F + 4 * H0) - 1).astype(jnp.int32),
        "send_fine": with_ends(jax.random.randint(splits[5], (PROWS, PCOLS, H0), 0, F // 2), jax.random.fold_in(splits[5], 1), 0, (F // 2) - 1).astype(jnp.int32),
        "prolong_fine": centred(splits[6], (PROWS, PCOLS, F, NODE, NODE), (4 * NODE) ** -0.5, 0.25, ((0, 4), (1, 8)), jnp.float32),
        "owner_fine": with_ends(jax.random.randint(splits[7], (PROWS, PCOLS, F), 0, F // 4), jax.random.fold_in(splits[7], 1), 0, (F // 4) - 1).astype(jnp.int32),
        "diag_mid": draw_diag_mid(jax.random.fold_in(splits[23], 71), 0),
        "couple_mid": centred(splits[9], (PROWS, PCOLS, MID, K, NODE, NODE), (16 * NODE) ** -0.5, 0.125, ((0, 4), (1, 8)), jnp.float32),
        "links_mid": with_ends(jax.random.randint(splits[10], (PROWS, PCOLS, MID, K), 0, MID + 4 * H1), jax.random.fold_in(splits[10], 1), 0, (MID + 4 * H1) - 1).astype(jnp.int32),
        "send_mid": with_ends(jax.random.randint(splits[11], (PROWS, PCOLS, H1), 0, MID), jax.random.fold_in(splits[11], 1), 0, MID - 1).astype(jnp.int32),
        "prolong_mid": centred(splits[12], (PROWS, PCOLS, MID, NODE, NODE), (2 * NODE) ** -0.5, 0.375, ((0, 4), (1, 8)), jnp.float32),
        "owner_mid": with_ends(jax.random.randint(splits[13], (PROWS, PCOLS, MID), 0, G2), jax.random.fold_in(splits[13], 1), 0, G2 - 1).astype(jnp.int32),
        "diag_row": draw_diag_row(jax.random.fold_in(splits[23], 71), 0),
        "couple_row": centred(splits[15], (PROWS, G2, K, NODE, NODE), (16 * NODE) ** -0.5, 0.125, ((0, 4),), jnp.float32),
        "links_row": with_ends(jax.random.randint(splits[16], (PROWS, G2, K), 0, G2 + 2 * H2), jax.random.fold_in(splits[16], 1), 0, (G2 + 2 * H2) - 1).astype(jnp.int32),
        "send_row": with_ends(jax.random.randint(splits[17], (PROWS, H2), 0, G2), jax.random.fold_in(splits[17], 1), 0, G2 - 1).astype(jnp.int32),
        "prolong_row": centred(splits[18], (PROWS, G2, NODE, NODE), (2 * NODE) ** -0.5, 0.375, ((0, 4),), jnp.float32),
        "owner_row": with_ends(jax.random.randint(splits[19], (PROWS, G2), 0, G3), jax.random.fold_in(splits[19], 1), 0, G3 - 1).astype(jnp.int32),
        "coarse_inverse": centred(splits[20], (G3 * NODE, G3 * NODE), (G3 * NODE) ** -0.5, 0.25, (), jnp.float32),
        "cheb_low": jnp.clip(jnp.exp(jax.random.uniform(splits[21], (LEVELS - 1,), jnp.float32, math.log(0.3), math.log(0.8))), 0.3, 0.8),
        "cheb_high": jnp.clip(jnp.exp(jax.random.uniform(splits[22], (LEVELS - 1,), jnp.float32, math.log(6.5), math.log(9.0))), 6.5, 9.0),
    }


HIGHEST = lax.Precision.HIGHEST


def chebyshev_terms(low_bound, high_bound):
    center_value = 0.5 * (high_bound + low_bound)
    half_width = 0.5 * (high_bound - low_bound)
    sigma_ratio = center_value / half_width
    first_rho = 1.0 / sigma_ratio
    second_rho = 1.0 / (2.0 * sigma_ratio - first_rho)
    return center_value, second_rho * first_rho, 2.0 * second_rho / half_width


def smooth(apply_fn, target, initial, cheb_terms, keep_last):
    center_value, carry_coef, gain_coef = cheb_terms
    if initial is None:
        residue = target
    else:
        residue = target - apply_fn(initial)
    update = residue / center_value
    if initial is None:
        solution = update
    else:
        solution = initial + update
    residue = residue - apply_fn(update)
    update = carry_coef * update + gain_coef * residue
    solution = solution + update
    if keep_last:
        residue = residue - apply_fn(update)
    return solution, residue


def block_apply(vector, diagonal, coupling, link_ids, send_ids, faces_fn):
    lead_dims = link_ids.ndim - 2
    sent_blocks = jnp.take_along_axis(vector, send_ids[..., None, None], axis=lead_dims)
    padded = faces_fn(sent_blocks)
    if lead_dims == 2:
        neighbours = [padded[:-2, 1:-1], padded[2:, 1:-1], padded[1:-1, :-2], padded[1:-1, 2:]]
    else:
        neighbours = [padded[:-2], padded[2:]]
    extended = jnp.concatenate([vector] + neighbours, axis=lead_dims)
    flat_links = link_ids.reshape(link_ids.shape[:lead_dims] + (-1,))
    picked = jnp.take_along_axis(extended, flat_links[..., None, None], axis=lead_dims)
    picked = picked.reshape(link_ids.shape + vector.shape[-2:])
    own_part = jnp.einsum("...brn,...bnm->...brm", vector, diagonal, precision=HIGHEST)
    far_part = jnp.einsum("...bkrn,...bknm->...brm", picked, coupling, precision=HIGHEST)
    return own_part + far_part


def restrict(residue, prolong, owners, block_count):
    pieces = jnp.einsum("...brf,...bcf->...brc", residue, prolong, precision=HIGHEST)
    one_hot = (owners[..., None] == jnp.arange(block_count, dtype=jnp.int32)).astype(jnp.float32)
    return jnp.einsum("...bc,...brn->...crn", one_hot, pieces, precision=HIGHEST)


def prolong_add(coarse, prolong, owners, block_count):
    one_hot = (owners[..., None] == jnp.arange(block_count, dtype=jnp.int32)).astype(jnp.float32)
    picked = jnp.einsum("...bc,...crn->...brn", one_hot, coarse, precision=HIGHEST)
    return jnp.einsum("...brc,...bcf->...brf", picked, prolong, precision=HIGHEST)


def coarse_solve(residue, inverse):
    num_blocks, num_sides, num_nodes = residue.shape
    flattened = jnp.transpose(residue, (1, 0, 2)).reshape(num_sides, num_blocks * num_nodes)
    solved = jnp.dot(flattened, inverse, precision=HIGHEST)
    return jnp.transpose(solved.reshape(num_sides, num_blocks, num_nodes), (1, 0, 2))


def grid_pad(sent_blocks):
    return jnp.pad(sent_blocks, ((1, 1), (1, 1), (0, 0), (0, 0), (0, 0)))


def row_pad(sent_blocks):
    return jnp.pad(sent_blocks, ((1, 1), (0, 0), (0, 0), (0, 0)))


def reference(right_side, live_blocks, diag_fine, couple_fine, links_fine, send_fine, prolong_fine, owner_fine, diag_mid, couple_mid, links_mid, send_mid, prolong_mid, owner_mid, diag_row, couple_row, links_row, send_row, prolong_row, owner_row, coarse_inverse, cheb_low, cheb_high):
    fine_count = diag_fine.shape[2]
    mid_count = diag_mid.shape[2]
    row_count = diag_row.shape[1]
    top_count = coarse_inverse.shape[0] // diag_row.shape[-1]
    live_mask = (jnp.arange(fine_count, dtype=jnp.int32)[None, None, :] < live_blocks[:, :, None]).astype(jnp.float32)[..., None, None]
    cheb_terms = [chebyshev_terms(cheb_low[level_index], cheb_high[level_index]) for level_index in range(3)]

    def apply_fine(vector):
        return block_apply(vector, diag_fine, couple_fine, links_fine, send_fine, grid_pad) * live_mask

    def apply_mid(vector):
        return block_apply(vector, diag_mid, couple_mid, links_mid, send_mid, grid_pad)

    def apply_row(vector):
        return block_apply(vector, diag_row, couple_row, links_row, send_row, row_pad)

    fine_target = right_side * live_mask
    fine_sol, fine_res = smooth(apply_fine, fine_target, None, cheb_terms[0], True)
    mid_target = restrict(fine_res, prolong_fine, owner_fine, mid_count)
    mid_sol, mid_res = smooth(apply_mid, mid_target, None, cheb_terms[1], True)
    row_target = jnp.sum(restrict(mid_res, prolong_mid, owner_mid, row_count), axis=1)
    row_sol, row_res = smooth(apply_row, row_target, None, cheb_terms[2], True)
    top_target = jnp.sum(restrict(row_res, prolong_row, owner_row, top_count), axis=0)
    top_sol = coarse_solve(top_target, coarse_inverse)
    spread_top = jnp.broadcast_to(top_sol[None], (row_sol.shape[0],) + top_sol.shape)
    row_sol = row_sol + prolong_add(spread_top, prolong_row, owner_row, top_count)
    row_sol, unused_row = smooth(apply_row, row_target, row_sol, cheb_terms[2], False)
    lifted = jnp.broadcast_to(row_sol[:, None], owner_mid.shape[:2] + row_sol.shape[1:])
    mid_sol = mid_sol + prolong_add(lifted, prolong_mid, owner_mid, row_count)
    mid_sol, unused_mid = smooth(apply_mid, mid_target, mid_sol, cheb_terms[1], False)
    fine_sol = fine_sol + prolong_add(mid_sol, prolong_fine, owner_fine, mid_count) * live_mask
    fine_sol, fine_res = smooth(apply_fine, fine_target, fine_sol, cheb_terms[0], True)
    return fine_sol, fine_res
```

```python
import functools

import jax
import jax.numpy as jnp
from jax import lax
from jax.experimental import pallas as pl
from jax.experimental.pallas import tpu as pltpu
from jax.sharding import PartitionSpec as P

MESH = pl.DeviceIdType.MESH
F32 = jnp.float32
BF16 = jnp.bfloat16


def halves(x):
    high = x.astype(BF16).astype(F32)
    return high, x - high


def rows_split(x):
    high, low = halves(x)
    return jnp.concatenate([high, low], axis=-2).astype(BF16)


def quarters(z):
    rows, cols = z.shape[0] // 2, z.shape[1] // 2
    folded = z[:, :cols] + z[:, cols:]
    return folded[:rows] + folded[rows:]


def kernel(
    npx,
    npy,
    live,
    links_fine,
    send_fine,
    owner_fine,
    links_mid,
    send_mid,
    owner_mid,
    links_row,
    send_row,
    owner_row,
    cheb_low,
    cheb_high,
    right_side,
    diag_fine,
    couple_fine,
    prolong_fine,
    diag_mid,
    couple_mid,
    prolong_mid,
    diag_row,
    couple_row,
    prolong_row,
    inverse,
    out_x,
    out_r,
    stage_df,
    stage_cf,
    stage_pf,
    stage_dm,
    stage_cm,
    stage_pm,
    stage_dr,
    stage_cr,
    stage_pr,
    stage_inv,
    w_df,
    w_cf,
    w_pf,
    w_dm,
    w_cm,
    w_pm,
    w_dr,
    w_cr,
    w_pr,
    w_inv,
    vec_f,
    ext_f,
    acc_f,
    vec_c,
    ext_c,
    acc_c,
    split_f,
    split_c,
    b_f,
    x_f,
    b_m,
    x_m,
    b_r,
    x_r,
    sbuf_f,
    rbuf_f,
    sbuf_m,
    rbuf_m,
    sbuf_r,
    rbuf_r,
    sum_y_src,
    sum_y,
    sum_x_src,
    sum_x,
    load_cf,
    load,
    ss_f,
    rs_f,
    ss_m,
    rs_m,
    ss_r,
    rs_r,
    ss_y,
    rs_y,
    ss_x,
    rs_x,
):
    px = lax.axis_index("px")
    py = lax.axis_index("py")
    fine = diag_fine.shape[0]
    mid = diag_mid.shape[0]
    row = diag_row.shape[0]
    node = diag_fine.shape[-1]
    top = inverse.shape[0] // node
    width_k = links_fine.shape[1]

    def couple_copy(b):
        return pltpu.make_async_copy(couple_fine.at[b], stage_cf.at[b], load_cf.at[b])

    def whole_copy(i):
        src, dst = (
            (diag_fine, stage_df),
            (prolong_fine, stage_pf),
            (diag_mid, stage_dm),
            (couple_mid, stage_cm),
            (prolong_mid, stage_pm),
            (diag_row, stage_dr),
            (couple_row, stage_cr),
            (prolong_row, stage_pr),
            (inverse, stage_inv),
        )[i]
        return pltpu.make_async_copy(src, dst, load.at[i])

    whole_copy(0).start()

    @pl.loop(0, fine)
    def _(b):
        couple_copy(b).start()

    for i in range(1, 9):
        whole_copy(i).start()

    barrier = pltpu.get_barrier_semaphore()
    for j in range(1, npx):
        pl.semaphore_signal(
            barrier, inc=1, device_id={"px": lax.rem(px + j, npx)}, device_id_type=MESH
        )
    for j in range(1, npy):
        pl.semaphore_signal(
            barrier, inc=1, device_id={"py": lax.rem(py + j, npy)}, device_id_type=MESH
        )

    has = (px > 0, px < npx - 1, py > 0, py < npy - 1)
    for d in range(4):

        @pl.when(jnp.logical_not(has[d]))
        def _(d=d):
            rbuf_f[:, d] = jnp.zeros(rbuf_f.shape[:1] + rbuf_f.shape[2:], F32)
            rbuf_m[:, d] = jnp.zeros(rbuf_m.shape[:1] + rbuf_m.shape[2:], F32)
            if d < 2:
                rbuf_r[:, d] = jnp.zeros(rbuf_r.shape[:1] + rbuf_r.shape[2:], F32)

    place = ({"px": px - 1}, {"px": px + 1}, {"py": py - 1}, {"py": py + 1})

    def halo_copy(bufs, e, d, target):
        src, dst, ss, rs = bufs
        return pltpu.make_async_remote_copy(
            src_ref=src.at[e],
            dst_ref=dst.at[e, d],
            send_sem=ss.at[e, d],
            recv_sem=rs.at[e, d],
            device_id=place[target],
            device_id_type=MESH,
        )

    def halo_start(bufs, e, dirs):
        for d in range(dirs):

            @pl.when(has[d ^ 1])
            def _(d=d):
                halo_copy(bufs, e, d, d ^ 1).start()

    def halo_recv(bufs, e, dirs):
        for d in range(dirs):

            @pl.when(has[d])
            def _(d=d):
                halo_copy(bufs, e, d, d).wait_recv()

    def halo_sent(bufs, count, dirs):
        for e in range(count):
            for d in range(dirs):

                @pl.when(has[d ^ 1])
                def _(d=d, e=e):
                    halo_copy(bufs, e, d, d ^ 1).wait_send()

    def sum_copy(axis, j):
        me, n, src, dst, ss, rs = (
            (px, npx, sum_x_src, sum_x, ss_x, rs_x)
            if axis == "px"
            else (py, npy, sum_y_src, sum_y, ss_y, rs_y)
        )
        return pltpu.make_async_remote_copy(
            src_ref=src,
            dst_ref=dst.at[j - 1],
            send_sem=ss.at[j - 1],
            recv_sem=rs.at[j - 1],
            device_id={axis: lax.rem(me + j, n)},
            device_id_type=MESH,
        )

    def all_sum(axis, n, src, dst, value):
        src[...] = value
        for j in range(1, n):
            sum_copy(axis, j).start()
        for j in range(1, n):
            sum_copy(axis, j).wait_recv()
        total = value
        for j in range(1, n):
            total = total + dst[j - 1]
        return total

    def split_cols(stage, w, b):
        high, low = halves(stage[b])
        w[b, :, :node] = high.astype(BF16)
        w[b, :, node:] = low.astype(BF16)

    def split_rows(stage, w, b):
        high, low = halves(stage[b])
        w[b, :node, :] = high.astype(BF16)
        w[b, node:, :] = low.astype(BF16)

    def split_all(i, stage, w, how):
        whole_copy(i).wait()

        @pl.loop(0, stage.shape[0])
        def _(b):
            how(stage, w, b)

    def split_couple_fine():
        @pl.loop(0, fine)
        def _(b):
            couple_copy(b).wait()
            split_cols(stage_cf, w_cf, b)

    def split_inverse():
        whole_copy(8).wait()
        size = inverse.shape[0]

        @pl.loop(0, size // node)
        def _(b):
            rows = pl.ds(pl.multiple_of(b * node, node), node)
            high, low = halves(stage_inv[rows, :])
            w_inv[rows, :size] = high.astype(BF16)
            w_inv[rows, size:] = low.astype(BF16)

    def apply(v, e, level, before_diag=None, before_couple=None):
        count, vec, ext, acc, bufs, dirs, links, send, w_d, w_c = level
        shared = send.shape[1]
        vec[:count] = v
        for h in range(shared):
            bufs[0][e, h] = vec[send[0, h]]
        halo_start(bufs, e, dirs)
        ext[:count] = rows_split(v)
        if before_diag is not None:
            before_diag()

        def own(b, carry):
            acc[b] = quarters(jnp.dot(ext[b], w_d[b], preferred_element_type=F32))
            return carry

        lax.fori_loop(0, count, own, 0, unroll=True)
        if before_couple is not None:
            before_couple()
        halo_recv(bufs, e, dirs)
        for d in range(dirs):
            ext[count + d * shared : count + (d + 1) * shared] = rows_split(bufs[1][e, d])

        def far(b, carry):
            picked = jnp.concatenate([ext[links[b, k]] for k in range(width_k)], axis=1)
            acc[b] += quarters(jnp.dot(picked, w_c[b], preferred_element_type=F32))
            return carry

        lax.fori_loop(0, count, far, 0, unroll=True)
        return acc[:count]

    def restrict(r, w_p, owner, count, groups, split):
        split[:count] = rows_split(r)
        totals = [jnp.zeros(r.shape[1:], F32) for _ in range(groups)]
        for b in range(count):
            piece = quarters(
                lax.dot_general(
                    split[b], w_p[b], (((1,), (1,)), ((), ())), preferred_element_type=F32
                )
            )
            for c in range(groups):
                totals[c] = totals[c] + piece * jnp.where(owner[0, b] == c, 1.0, 0.0)
        return jnp.stack(totals)

    def prolong(u, w_p, owner, count, split):
        split[: u.shape[0]] = rows_split(u)
        out = []
        for b in range(count):
            part = split[owner[0, b]]
            z = jnp.dot(
                jnp.concatenate([part, part], axis=1), w_p[b], preferred_element_type=F32
            )
            out.append(z[: z.shape[0] // 2] + z[z.shape[0] // 2 :])
        return jnp.stack(out)

    def terms(level):
        shape = right_side.shape[1:]
        low = jnp.full(shape, cheb_low[level], F32)
        high = jnp.full(shape, cheb_high[level], F32)
        center = 0.5 * (high + low)
        half_width = 0.5 * (high - low)
        ratio = center / half_width
        first = 1.0 / ratio
        second = 1.0 / (2.0 * ratio - first)
        return (1.0 / center)[None], (second * first)[None], (2.0 * second / half_width)[None]

    bufs_f = (sbuf_f, rbuf_f, ss_f, rs_f)
    bufs_m = (sbuf_m, rbuf_m, ss_m, rs_m)
    bufs_r = (sbuf_r, rbuf_r, ss_r, rs_r)
    level_f = (fine, vec_f, ext_f, acc_f, bufs_f, 4, links_fine, send_fine, w_df, w_cf)
    level_m = (mid, vec_c, ext_c, acc_c, bufs_m, 4, links_mid, send_mid, w_dm, w_cm)
    level_r = (row, vec_c, ext_c, acc_c, bufs_r, 2, links_row, send_row, w_dr, w_cr)

    mask = jnp.where(
        lax.broadcasted_iota(jnp.int32, right_side.shape, 0) < live[0, 0], 1.0, 0.0
    ).astype(F32)

    inv_c, carry_c, gain_c = terms(0)
    target = right_side[...] * mask
    b_f[...] = target
    d = target * inv_c
    pl.semaphore_wait(barrier, npx + npy - 2)
    ad = apply(
        d,
        0,
        level_f,
        before_diag=lambda: split_all(0, stage_df, w_df, split_cols),
        before_couple=split_couple_fine,
    )
    r = target - ad * mask
    d2 = carry_c * d + gain_c * r
    x_f[...] = d + d2

    def more():
        split_all(1, stage_pf, w_pf, split_rows)
        split_all(2, stage_dm, w_dm, split_cols)
        split_all(3, stage_cm, w_cm, split_cols)

    r = r - apply(d2, 1, level_f, before_couple=more) * mask

    inv_c, carry_c, gain_c = terms(1)
    target = restrict(r, w_pf, owner_fine, fine, mid, split_f)
    b_m[...] = target
    d = target * inv_c
    r = target - apply(
        d, 0, level_m, before_couple=lambda: split_all(4, stage_pm, w_pm, split_rows)
    )
    d2 = carry_c * d + gain_c * r
    x_m[...] = d + d2

    def row_split():
        split_all(5, stage_dr, w_dr, split_cols)
        split_all(6, stage_cr, w_cr, split_cols)
        split_all(7, stage_pr, w_pr, split_rows)

    r = r - apply(d2, 1, level_m, before_couple=row_split)

    inv_c, carry_c, gain_c = terms(2)
    share = restrict(r, w_pm, owner_mid, mid, row, split_c)
    target = all_sum("py", npy, sum_y_src, sum_y, share)
    b_r[...] = target
    d = target * inv_c
    r = target - apply(d, 0, level_r, before_couple=split_inverse)
    d2 = carry_c * d + gain_c * r
    x_r[...] = d + d2
    r = r - apply(d2, 1, level_r)

    part = restrict(r, w_pr, owner_row, row, top, split_c)
    top_target = all_sum("px", npx, sum_x_src, sum_x, part)
    flat = jnp.concatenate([rows_split(top_target[c]) for c in range(top)], axis=1)
    solved = quarters(jnp.dot(flat, w_inv[...], preferred_element_type=F32))
    top_sol = jnp.stack([solved[:, c * node : (c + 1) * node] for c in range(top)])

    x = x_r[...] + prolong(top_sol, w_pr, owner_row, row, split_c)
    x_r[...] = x
    r = b_r[...] - apply(x, 2, level_r)
    d = r * inv_c
    x_r[...] += d
    r = r - apply(d, 3, level_r)
    x = x_r[...] + carry_c * d + gain_c * r

    inv_c, carry_c, gain_c = terms(1)
    x = x_m[...] + prolong(x, w_pm, owner_mid, mid, split_c)
    x_m[...] = x
    r = b_m[...] - apply(x, 2, level_m)
    d = r * inv_c
    x_m[...] += d
    r = r - apply(d, 3, level_m)
    x = x_m[...] + carry_c * d + gain_c * r

    inv_c, carry_c, gain_c = terms(0)
    x = x_f[...] + prolong(x, w_pf, owner_fine, fine, split_c) * mask
    x_f[...] = x
    r = b_f[...] - apply(x, 2, level_f) * mask
    d = r * inv_c
    x_f[...] += d
    r = r - apply(d, 3, level_f) * mask
    d2 = carry_c * d + gain_c * r
    out_x[...] = x_f[...] + d2
    out_r[...] = r - apply(d2, 4, level_f) * mask

    halo_sent(bufs_f, rbuf_f.shape[0], 4)
    halo_sent(bufs_m, rbuf_m.shape[0], 4)
    halo_sent(bufs_r, rbuf_r.shape[0], 2)
    for j in range(1, npy):
        sum_copy("py", j).wait_send()
    for j in range(1, npx):
        sum_copy("px", j).wait_send()


def body(
    right_side,
    live_blocks,
    diag_fine,
    couple_fine,
    links_fine,
    send_fine,
    prolong_fine,
    owner_fine,
    diag_mid,
    couple_mid,
    links_mid,
    send_mid,
    prolong_mid,
    owner_mid,
    diag_row,
    couple_row,
    links_row,
    send_row,
    prolong_row,
    owner_row,
    coarse_inverse,
    cheb_low,
    cheb_high,
):
    npx, npy = lax.axis_size("px"), lax.axis_size("py")
    fine, sides, node = right_side.shape[2:]
    mid = diag_mid.shape[2]
    row = diag_row.shape[1]
    k = couple_fine.shape[3]
    size = coarse_inverse.shape[0]
    top = size // node
    h0, h1, h2 = send_fine.shape[-1], send_mid.shape[-1], send_row.shape[-1]
    coarse_most = max(mid, row, top)
    ext_most = max(mid + 4 * h1, row + 2 * h2)

    scalars = (
        live_blocks,
        links_fine.reshape(fine, k),
        send_fine.reshape(1, h0),
        owner_fine.reshape(1, fine),
        links_mid.reshape(mid, k),
        send_mid.reshape(1, h1),
        owner_mid.reshape(1, mid),
        links_row.reshape(row, k),
        send_row,
        owner_row,
        cheb_low,
        cheb_high,
    )
    arrays = (
        diag_fine.reshape(fine, node, node),
        couple_fine.reshape(fine, k * node, node),
        prolong_fine.reshape(fine, node, node),
        diag_mid.reshape(mid, node, node),
        couple_mid.reshape(mid, k * node, node),
        prolong_mid.reshape(mid, node, node),
        diag_row.reshape(row, node, node),
        couple_row.reshape(row, k * node, node),
        prolong_row.reshape(row, node, node),
        coarse_inverse,
    )
    vm = pltpu.VMEM
    dma = pltpu.SemaphoreType.DMA
    scratch = [vm(a.shape, F32) for a in arrays]
    for count in (fine, mid, row):
        scratch += [
            vm((count, node, 2 * node), BF16),
            vm((count, k * node, 2 * node), BF16),
            vm((count, 2 * node, node), BF16),
        ]
    scratch.append(vm((size, 2 * size), BF16))
    scratch += [
        vm((fine, sides, node), F32),
        vm((fine + 4 * h0, 2 * sides, node), BF16),
        vm((fine, sides, node), F32),
        vm((coarse_most, sides, node), F32),
        vm((ext_most, 2 * sides, node), BF16),
        vm((coarse_most, sides, node), F32),
        vm((fine, 2 * sides, node), BF16),
        vm((coarse_most, 2 * sides, node), BF16),
    ]
    for count in (fine, mid, row):
        scratch += [vm((count, sides, node), F32)] * 2
    for uses, dirs, shared in ((5, 4, h0), (4, 4, h1), (4, 2, h2)):
        scratch += [
            vm((uses, shared, sides, node), F32),
            vm((uses, dirs, shared, sides, node), F32),
        ]
    scratch += [
        vm((row, sides, node), F32),
        vm((npy - 1, row, sides, node), F32),
        vm((top, sides, node), F32),
        vm((npx - 1, top, sides, node), F32),
        dma((fine,)),
        dma((9,)),
    ]
    for uses, dirs in ((5, 4), (4, 4), (4, 2)):
        scratch += [dma((uses, dirs))] * 2
    scratch += [dma((npy - 1,))] * 2 + [dma((npx - 1,))] * 2

    shape = jax.ShapeDtypeStruct((fine, sides, node), F32)
    products = fine * (k + 1) * 5 + (mid + row) * (k + 1) * 4 + 2 * (fine + mid + row) + 16
    sol, res = pl.pallas_call(
        functools.partial(kernel, npx, npy),
        out_shape=(shape, shape),
        in_specs=[pl.BlockSpec(memory_space=pltpu.SMEM)] * len(scalars)
        + [pl.BlockSpec(memory_space=pltpu.VMEM)]
        + [pl.BlockSpec(memory_space=pl.ANY)] * len(arrays),
        out_specs=(pl.BlockSpec(memory_space=pltpu.VMEM),) * 2,
        scratch_shapes=scratch,
        compiler_params=pltpu.CompilerParams(
            collective_id=0, has_side_effects=True, vmem_limit_bytes=48 * 1024 * 1024
        ),
        cost_estimate=pl.CostEstimate(
            flops=products * 2 * sides * node * node * 4,
            bytes_accessed=sum(4 * a.size for a in arrays),
            transcendentals=0,
        ),
        name="vcycle",
    )(*scalars, right_side.reshape(fine, sides, node), *arrays)
    full = (1, 1, fine, sides, node)
    return sol.reshape(full), res.reshape(full)


def solution(mesh):
    grid = P("px", "py")
    line = P("px")
    whole = P()
    return jax.shard_map(
        body,
        mesh=mesh,
        in_specs=(grid,) * 14 + (line,) * 6 + (whole,) * 3,
        out_specs=(grid, grid),
        check_vma=False,
    )
```

```python
import functools

import jax
import jax.numpy as jnp
from jax import lax
from jax.experimental import pallas as pl
from jax.experimental.pallas import tpu as pltpu
from jax.sharding import PartitionSpec as P

MESH = pl.DeviceIdType.MESH
F32 = jnp.float32
BF16 = jnp.bfloat16


def halves(x):
    high = x.astype(BF16).astype(F32)
    return high, x - high


def rows_split(x):
    high, low = halves(x)
    return jnp.concatenate([high, low], axis=-2).astype(BF16)


def quarters(z):
    rows, cols = z.shape[0] // 2, z.shape[1] // 2
    folded = z[:, :cols] + z[:, cols:]
    return folded[:rows] + folded[rows:]


def kernel(
    npx,
    npy,
    *refs,
):
    scalars_hbm, refs = refs[:12], refs[12:]
    scalars, refs = refs[-13:-1], refs[:-13] + refs[-1:]
    (
        live,
        links_fine,
        send_fine,
        owner_fine,
        links_mid,
        send_mid,
        owner_mid,
        links_row,
        send_row,
        owner_row,
        cheb_low,
        cheb_high,
    ) = scalars
    (
    right_hbm,
    diag_fine,
    couple_fine,
    prolong_fine,
    diag_mid,
    couple_mid,
    prolong_mid,
    diag_row,
    couple_row,
    prolong_row,
    inverse,
    out,
    stage_df,
    stage_cf,
    stage_pf,
    stage_dm,
    stage_cm,
    stage_pm,
    stage_dr,
    stage_cr,
    stage_pr,
    stage_inv,
    w_df,
    w_cf,
    w_pf,
    w_dm,
    w_cm,
    w_pm,
    w_dr,
    w_cr,
    w_pr,
    w_inv,
    vec_f,
    ext_f,
    acc_f,
    vec_c,
    ext_c,
    acc_c,
    split_f,
    split_c,
    b_f,
    x_f,
    b_m,
    x_m,
    b_r,
    x_r,
    sbuf_f,
    rbuf_f,
    sbuf_m,
    rbuf_m,
    sbuf_r,
    rbuf_r,
    sum_y_src,
    sum_y,
    sum_x_src,
    sum_x,
    load_cf,
    load,
    ss_f,
    rs_f,
    ss_m,
    rs_m,
    ss_r,
    rs_r,
    ss_y,
    rs_y,
    ss_x,
    rs_x,
    right_side,
    load_s,
    ) = refs
    px = lax.axis_index("px")
    py = lax.axis_index("py")
    fine = diag_fine.shape[0]
    mid = diag_mid.shape[0]
    row = diag_row.shape[0]
    node = diag_fine.shape[-1]
    top = inverse.shape[0] // node
    width_k = links_mid.shape[1]

    barrier = pltpu.get_barrier_semaphore()
    for j in range(1, npx):
        pl.semaphore_signal(
            barrier, inc=1, device_id={"px": lax.rem(px + j, npx)}, device_id_type=MESH
        )
    for j in range(1, npy):
        pl.semaphore_signal(
            barrier, inc=1, device_id={"py": lax.rem(py + j, npy)}, device_id_type=MESH
        )

    parts = load_cf.shape[0]
    per_part = fine // parts

    def couple_copy(i):
        blocks = pl.ds(i * per_part, per_part)
        return pltpu.make_async_copy(couple_fine.at[blocks], stage_cf.at[blocks], load_cf.at[i])

    def whole_copy(i):
        src, dst = (
            (diag_fine, stage_df),
            (prolong_fine, stage_pf),
            (diag_mid, stage_dm),
            (couple_mid, stage_cm),
            (prolong_mid, stage_pm),
            (diag_row, stage_dr),
            (couple_row, stage_cr),
            (prolong_row, stage_pr),
            (inverse, stage_inv),
        )[i]
        return pltpu.make_async_copy(src, dst, load.at[i])

    small = [
        pltpu.make_async_copy(src, dst, load_s.at[i])
        for i, (src, dst) in enumerate(
            zip(scalars_hbm + (right_hbm,), scalars + (right_side,))
        )
    ]
    for copy in small:
        copy.start()
    whole_copy(0).start()

    for i in range(parts):
        couple_copy(i).start()

    for i in range(1, 9):
        whole_copy(i).start()

    has = (px > 0, px < npx - 1, py > 0, py < npy - 1)
    for d in range(4):

        @pl.when(jnp.logical_not(has[d]))
        def _(d=d):
            rbuf_f[:, d] = jnp.zeros(rbuf_f.shape[:1] + rbuf_f.shape[2:], F32)
            rbuf_m[:, d] = jnp.zeros(rbuf_m.shape[:1] + rbuf_m.shape[2:], F32)
            if d < 2:
                rbuf_r[:, d] = jnp.zeros(rbuf_r.shape[:1] + rbuf_r.shape[2:], F32)

    place = ({"px": px - 1}, {"px": px + 1}, {"py": py - 1}, {"py": py + 1})

    def halo_copy(bufs, e, d, target):
        src, dst, ss, rs = bufs
        return pltpu.make_async_remote_copy(
            src_ref=src.at[e],
            dst_ref=dst.at[e, d],
            send_sem=ss.at[e, d],
            recv_sem=rs.at[e, d],
            device_id=place[target],
            device_id_type=MESH,
        )

    def halo_start(bufs, e, dirs):
        for d in reversed(range(dirs)):

            @pl.when(has[d ^ 1])
            def _(d=d):
                halo_copy(bufs, e, d, d ^ 1).start()

    def halo_recv(bufs, e, dirs):
        for d in range(dirs):

            @pl.when(has[d])
            def _(d=d):
                halo_copy(bufs, e, d, d).wait_recv()

    def halo_sent(bufs, count, dirs):
        for e in range(count):
            for d in range(dirs):

                @pl.when(has[d ^ 1])
                def _(d=d, e=e):
                    halo_copy(bufs, e, d, d ^ 1).wait_send()

    def sum_copy(axis, j):
        me, n, src, dst, ss, rs = (
            (px, npx, sum_x_src, sum_x, ss_x, rs_x)
            if axis == "px"
            else (py, npy, sum_y_src, sum_y, ss_y, rs_y)
        )
        return pltpu.make_async_remote_copy(
            src_ref=src,
            dst_ref=dst.at[j - 1],
            send_sem=ss.at[j - 1],
            recv_sem=rs.at[j - 1],
            device_id={axis: lax.rem(me + j, n)},
            device_id_type=MESH,
        )

    def all_sum(axis, n, src, dst, value):
        src[...] = value
        for j in range(1, n):
            sum_copy(axis, j).start()
        for j in range(1, n):
            sum_copy(axis, j).wait_recv()
        total = value
        for j in range(1, n):
            total = total + dst[j - 1]
        return total

    def split_cols(stage, w, b):
        high, low = halves(stage[b])
        w[b, :, :node] = high.astype(BF16)
        w[b, :, node:] = low.astype(BF16)

    def split_rows(stage, w, b):
        high, low = halves(stage[b])
        w[b, :node, :] = high.astype(BF16)
        w[b, node:, :] = low.astype(BF16)

    def split_all(i, stage, w, how):
        whole_copy(i).wait()

        @pl.loop(0, stage.shape[0])
        def _(b):
            how(stage, w, b)

    def split_couple_fine():
        for i in range(parts):
            couple_copy(i).wait()

            @pl.loop(i * per_part, (i + 1) * per_part)
            def _(b):
                split_cols(stage_cf, w_cf, b)

    def split_inverse():
        whole_copy(8).wait()
        size = inverse.shape[0]

        @pl.loop(0, size // node)
        def _(b):
            rows = pl.ds(pl.multiple_of(b * node, node), node)
            high, low = halves(stage_inv[rows, :])
            w_inv[rows, :size] = high.astype(BF16)
            w_inv[rows, size:] = low.astype(BF16)

    def apply(v, e, level, before_diag=None, before_couple=None):
        count, vec, ext, acc, bufs, dirs, links, send, w_d, w_c = level
        shared = send.shape[1]
        vec[:count] = v
        for h in range(shared):
            bufs[0][e, h] = vec[send[0, h]]
        halo_start(bufs, e, dirs)
        ext[:count] = rows_split(v)
        if before_diag is not None:
            before_diag()

        def own(b, carry):
            acc[b] = quarters(jnp.dot(ext[b], w_d[b], preferred_element_type=F32))
            return carry

        lax.fori_loop(0, count, own, 0, unroll=True)
        if before_couple is not None:
            before_couple()
        halo_recv(bufs, e, dirs)
        for d in range(dirs):
            ext[count + d * shared : count + (d + 1) * shared] = rows_split(bufs[1][e, d])

        def far(b, carry):
            picked = jnp.concatenate([ext[links(b, k)] for k in range(width_k)], axis=1)
            acc[b] += quarters(jnp.dot(picked, w_c[b], preferred_element_type=F32))
            return carry

        lax.fori_loop(0, count, far, 0, unroll=True)
        return acc[:count]

    def restrict(r, w_p, owner, count, groups, split):
        split[:count] = rows_split(r)
        totals = [jnp.zeros(r.shape[1:], F32) for _ in range(groups)]
        for b in range(count):
            piece = quarters(
                lax.dot_general(
                    split[b], w_p[b], (((1,), (1,)), ((), ())), preferred_element_type=F32
                )
            )
            for c in range(groups):
                totals[c] = totals[c] + piece * jnp.where(owner[0, b] == c, 1.0, 0.0)
        return jnp.stack(totals)

    def prolong(u, w_p, owner, count, split):
        split[: u.shape[0]] = rows_split(u)
        out = []
        for b in range(count):
            part = split[owner[0, b]]
            z = jnp.dot(
                jnp.concatenate([part, part], axis=1), w_p[b], preferred_element_type=F32
            )
            out.append(z[: z.shape[0] // 2] + z[z.shape[0] // 2 :])
        return jnp.stack(out)

    def terms(level):
        shape = out.shape[2:]
        low = jnp.full(shape, cheb_low[level], F32)
        high = jnp.full(shape, cheb_high[level], F32)
        center = 0.5 * (high + low)
        half_width = 0.5 * (high - low)
        ratio = center / half_width
        first = 1.0 / ratio
        second = 1.0 / (2.0 * ratio - first)
        return (1.0 / center)[None], (second * first)[None], (2.0 * second / half_width)[None]

    bufs_f = (sbuf_f, rbuf_f, ss_f, rs_f)
    bufs_m = (sbuf_m, rbuf_m, ss_m, rs_m)
    bufs_r = (sbuf_r, rbuf_r, ss_r, rs_r)
    level_f = (fine, vec_f, ext_f, acc_f, bufs_f, 4, lambda b, k: links_fine[k, b], send_fine, w_df, w_cf)
    level_m = (mid, vec_c, ext_c, acc_c, bufs_m, 4, lambda b, k: links_mid[b, k], send_mid, w_dm, w_cm)
    level_r = (row, vec_c, ext_c, acc_c, bufs_r, 2, lambda b, k: links_row[b, k], send_row, w_dr, w_cr)

    for copy in small:
        copy.wait()
    mask = jnp.where(
        lax.broadcasted_iota(jnp.int32, right_side.shape, 0) < live[0, 0], 1.0, 0.0
    ).astype(F32)

    inv_c, carry_c, gain_c = terms(0)
    target = right_side[...] * mask
    b_f[...] = target
    d = target * inv_c
    pl.semaphore_wait(barrier, npx + npy - 2)
    ad = apply(
        d,
        0,
        level_f,
        before_diag=lambda: split_all(0, stage_df, w_df, split_cols),
        before_couple=split_couple_fine,
    )
    r = target - ad * mask
    d2 = carry_c * d + gain_c * r
    x_f[...] = d + d2

    def more():
        split_all(1, stage_pf, w_pf, split_rows)
        split_all(2, stage_dm, w_dm, split_cols)
        split_all(3, stage_cm, w_cm, split_cols)

    r = r - apply(d2, 1, level_f, before_couple=more) * mask

    inv_c, carry_c, gain_c = terms(1)
    target = restrict(r, w_pf, owner_fine, fine, mid, split_f)
    b_m[...] = target
    d = target * inv_c
    r = target - apply(
        d, 0, level_m, before_couple=lambda: split_all(4, stage_pm, w_pm, split_rows)
    )
    d2 = carry_c * d + gain_c * r
    x_m[...] = d + d2

    def row_split():
        split_all(5, stage_dr, w_dr, split_cols)
        split_all(6, stage_cr, w_cr, split_cols)
        split_all(7, stage_pr, w_pr, split_rows)

    r = r - apply(d2, 1, level_m, before_couple=row_split)

    inv_c, carry_c, gain_c = terms(2)
    share = restrict(r, w_pm, owner_mid, mid, row, split_c)
    target = all_sum("py", npy, sum_y_src, sum_y, share)
    b_r[...] = target
    d = target * inv_c
    r = target - apply(d, 0, level_r, before_couple=split_inverse)
    d2 = carry_c * d + gain_c * r
    x_r[...] = d + d2
    r = r - apply(d2, 1, level_r)

    part = restrict(r, w_pr, owner_row, row, top, split_c)
    top_target = all_sum("px", npx, sum_x_src, sum_x, part)
    flat = jnp.concatenate([rows_split(top_target[c]) for c in range(top)], axis=1)
    solved = quarters(jnp.dot(flat, w_inv[...], preferred_element_type=F32))
    top_sol = jnp.stack([solved[:, c * node : (c + 1) * node] for c in range(top)])

    x = x_r[...] + prolong(top_sol, w_pr, owner_row, row, split_c)
    x_r[...] = x
    r = b_r[...] - apply(x, 2, level_r)
    d = r * inv_c
    x_r[...] += d
    r = r - apply(d, 3, level_r)
    x = x_r[...] + carry_c * d + gain_c * r

    inv_c, carry_c, gain_c = terms(1)
    x = x_m[...] + prolong(x, w_pm, owner_mid, mid, split_c)
    x_m[...] = x
    r = b_m[...] - apply(x, 2, level_m)
    d = r * inv_c
    x_m[...] += d
    r = r - apply(d, 3, level_m)
    x = x_m[...] + carry_c * d + gain_c * r

    inv_c, carry_c, gain_c = terms(0)
    x = x_f[...] + prolong(x, w_pf, owner_fine, fine, split_c) * mask
    x_f[...] = x
    r = b_f[...] - apply(x, 2, level_f) * mask
    d = r * inv_c
    x_f[...] += d
    r = r - apply(d, 3, level_f) * mask
    d2 = carry_c * d + gain_c * r
    out[0] = x_f[...] + d2
    out[1] = r - apply(d2, 4, level_f) * mask

    halo_sent(bufs_f, rbuf_f.shape[0], 4)
    halo_sent(bufs_m, rbuf_m.shape[0], 4)
    halo_sent(bufs_r, rbuf_r.shape[0], 2)
    for j in range(1, npy):
        sum_copy("py", j).wait_send()
    for j in range(1, npx):
        sum_copy("px", j).wait_send()


def body(
    right_side,
    live_blocks,
    diag_fine,
    couple_fine,
    links_fine,
    send_fine,
    prolong_fine,
    owner_fine,
    diag_mid,
    couple_mid,
    links_mid,
    send_mid,
    prolong_mid,
    owner_mid,
    diag_row,
    couple_row,
    links_row,
    send_row,
    prolong_row,
    owner_row,
    coarse_inverse,
    cheb_low,
    cheb_high,
):
    npx, npy = lax.axis_size("px"), lax.axis_size("py")
    fine, sides, node = right_side.shape[2:]
    mid = diag_mid.shape[2]
    row = diag_row.shape[1]
    k = couple_fine.shape[3]
    size = coarse_inverse.shape[0]
    top = size // node
    h0, h1, h2 = send_fine.shape[-1], send_mid.shape[-1], send_row.shape[-1]
    coarse_most = max(mid, row, top)
    ext_most = max(mid + 4 * h1, row + 2 * h2)

    scalars = (
        live_blocks,
        jnp.swapaxes(links_fine.reshape(fine, k), 0, 1),
        send_fine.reshape(1, h0),
        owner_fine.reshape(1, fine),
        links_mid.reshape(mid, k),
        send_mid.reshape(1, h1),
        owner_mid.reshape(1, mid),
        links_row.reshape(row, k),
        send_row,
        owner_row,
        cheb_low,
        cheb_high,
    )
    arrays = (
        diag_fine.reshape(fine, node, node),
        couple_fine.reshape(fine, k * node, node),
        prolong_fine.reshape(fine, node, node),
        diag_mid.reshape(mid, node, node),
        couple_mid.reshape(mid, k * node, node),
        prolong_mid.reshape(mid, node, node),
        diag_row.reshape(row, node, node),
        couple_row.reshape(row, k * node, node),
        prolong_row.reshape(row, node, node),
        coarse_inverse,
    )
    vm = pltpu.VMEM
    dma = pltpu.SemaphoreType.DMA
    scratch = [vm(a.shape, F32) for a in arrays]
    for count in (fine, mid, row):
        scratch += [
            vm((count, node, 2 * node), BF16),
            vm((count, k * node, 2 * node), BF16),
            vm((count, 2 * node, node), BF16),
        ]
    scratch.append(vm((size, 2 * size), BF16))
    scratch += [
        vm((fine, sides, node), F32),
        vm((fine + 4 * h0, 2 * sides, node), BF16),
        vm((fine, sides, node), F32),
        vm((coarse_most, sides, node), F32),
        vm((ext_most, 2 * sides, node), BF16),
        vm((coarse_most, sides, node), F32),
        vm((fine, 2 * sides, node), BF16),
        vm((coarse_most, 2 * sides, node), BF16),
    ]
    for count in (fine, mid, row):
        scratch += [vm((count, sides, node), F32)] * 2
    for uses, dirs, shared in ((5, 4, h0), (4, 4, h1), (4, 2, h2)):
        scratch += [
            vm((uses, shared, sides, node), F32),
            vm((uses, dirs, shared, sides, node), F32),
        ]
    scratch += [
        vm((row, sides, node), F32),
        vm((npy - 1, row, sides, node), F32),
        vm((top, sides, node), F32),
        vm((npx - 1, top, sides, node), F32),
        dma((4 if fine % 4 == 0 else 1,)),
        dma((9,)),
    ]
    for uses, dirs in ((5, 4), (4, 4), (4, 2)):
        scratch += [dma((uses, dirs))] * 2
    scratch += [dma((npy - 1,))] * 2 + [dma((npx - 1,))] * 2
    scratch.append(vm((fine, sides, node), F32))
    scratch += [pltpu.SMEM(a.shape, a.dtype) for a in scalars]
    scratch.append(dma((len(scalars) + 1,)))

    shape = jax.ShapeDtypeStruct((2, fine, sides, node), F32)
    products = fine * (k + 1) * 5 + (mid + row) * (k + 1) * 4 + 2 * (fine + mid + row) + 16
    out = pl.pallas_call(
        functools.partial(kernel, npx, npy),
        out_shape=shape,
        in_specs=[pl.BlockSpec(memory_space=pltpu.HBM)] * (len(scalars) + 1 + len(arrays)),
        out_specs=pl.BlockSpec(memory_space=pltpu.VMEM),
        scratch_shapes=scratch,
        compiler_params=pltpu.CompilerParams(
            collective_id=0, has_side_effects=True, vmem_limit_bytes=56 * 1024 * 1024
        ),
        cost_estimate=pl.CostEstimate(
            flops=products * 2 * sides * node * node * 4,
            bytes_accessed=sum(4 * a.size for a in arrays),
            transcendentals=0,
        ),
        name="vcycle",
    )(*scalars, right_side.reshape(fine, sides, node), *arrays)
    full = (1, 1, fine, sides, node)
    return out[0].reshape(full), out[1].reshape(full)


def solution(mesh):
    grid = P("px", "py")
    line = P("px")
    whole = P()
    return jax.shard_map(
        body,
        mesh=mesh,
        in_specs=(grid,) * 14 + (line,) * 6 + (whole,) * 3,
        out_specs=(grid, grid),
        check_vma=False,
    )
```

```python
import functools

import jax
import jax.numpy as jnp
from jax import lax
from jax.experimental import pallas as pl
from jax.experimental.pallas import tpu as pltpu
from jax.sharding import PartitionSpec as P

MESH = pl.DeviceIdType.MESH
F32 = jnp.float32
BF16 = jnp.bfloat16


def halves(x):
    high = x.astype(BF16).astype(F32)
    return high, x - high


def rows_split(x):
    high, low = halves(x)
    return jnp.concatenate([high, low], axis=-2).astype(BF16)


def quarters(z):
    rows, cols = z.shape[0] // 2, z.shape[1] // 2
    folded = z[:, :cols] + z[:, cols:]
    return folded[:rows] + folded[rows:]


def kernel(
    npx,
    npy,
    *refs,
):
    scalars_hbm, refs = refs[:12], refs[12:]
    scalars, refs = refs[-13:-1], refs[:-13] + refs[-1:]
    (
        live,
        links_fine,
        send_fine,
        owner_fine,
        links_mid,
        send_mid,
        owner_mid,
        links_row,
        send_row,
        owner_row,
        cheb_low,
        cheb_high,
    ) = scalars
    (
    right_hbm,
    diag_fine,
    couple_fine,
    prolong_fine,
    diag_mid,
    couple_mid,
    prolong_mid,
    diag_row,
    couple_row,
    prolong_row,
    inverse,
    out,
    stage_df,
    stage_cf,
    stage_pf,
    stage_dm,
    stage_cm,
    stage_pm,
    stage_dr,
    stage_cr,
    stage_pr,
    stage_inv,
    w_df,
    w_cf,
    w_pf,
    w_dm,
    w_cm,
    w_pm,
    w_dr,
    w_cr,
    w_pr,
    w_inv,
    vec_f,
    ext_f,
    acc_f,
    vec_c,
    ext_c,
    acc_c,
    split_f,
    split_c,
    b_f,
    x_f,
    b_m,
    x_m,
    b_r,
    x_r,
    sbuf_f,
    rbuf_f,
    sbuf_m,
    rbuf_m,
    sbuf_r,
    rbuf_r,
    sum_y_src,
    sum_y,
    sum_x_src,
    sum_x,
    load_cf,
    load,
    ss_f,
    rs_f,
    ss_m,
    rs_m,
    ss_r,
    rs_r,
    ss_y,
    rs_y,
    ss_x,
    rs_x,
    right_side,
    load_s,
    ) = refs
    px = lax.axis_index("px")
    py = lax.axis_index("py")
    fine = diag_fine.shape[0]
    mid = diag_mid.shape[0]
    row = diag_row.shape[0]
    node = diag_fine.shape[-1]
    top = inverse.shape[0] // node
    width_k = links_mid.shape[1]

    barrier = pltpu.get_barrier_semaphore()
    for j in range(1, npx):
        pl.semaphore_signal(
            barrier, inc=1, device_id={"px": lax.rem(px + j, npx)}, device_id_type=MESH
        )
    for j in range(1, npy):
        pl.semaphore_signal(
            barrier, inc=1, device_id={"py": lax.rem(py + j, npy)}, device_id_type=MESH
        )

    parts = load_cf.shape[0]
    per_part = fine // parts

    def couple_copy(i):
        blocks = pl.ds(i * per_part, per_part)
        return pltpu.make_async_copy(couple_fine.at[blocks], stage_cf.at[blocks], load_cf.at[i])

    def whole_copy(i):
        src, dst = (
            (diag_fine, stage_df),
            (prolong_fine, stage_pf),
            (diag_mid, stage_dm),
            (couple_mid, stage_cm),
            (prolong_mid, stage_pm),
            (diag_row, stage_dr),
            (couple_row, stage_cr),
            (prolong_row, stage_pr),
            (inverse, stage_inv),
        )[i]
        return pltpu.make_async_copy(src, dst, load.at[i])

    small = [
        pltpu.make_async_copy(src, dst, load_s.at[i])
        for i, (src, dst) in enumerate(
            zip(scalars_hbm + (right_hbm,), scalars + (right_side,))
        )
    ]
    for copy in small:
        copy.start()
    whole_copy(0).start()

    for i in range(parts):
        couple_copy(i).start()

    for i in range(1, 9):
        whole_copy(i).start()

    has = (px > 0, px < npx - 1, py > 0, py < npy - 1)
    for d in range(4):

        @pl.when(jnp.logical_not(has[d]))
        def _(d=d):
            rbuf_f[:, d] = jnp.zeros(rbuf_f.shape[:1] + rbuf_f.shape[2:], F32)
            rbuf_m[:, d] = jnp.zeros(rbuf_m.shape[:1] + rbuf_m.shape[2:], F32)
            if d < 2:
                rbuf_r[:, d] = jnp.zeros(rbuf_r.shape[:1] + rbuf_r.shape[2:], F32)

    place = ({"px": px - 1}, {"px": px + 1}, {"py": py - 1}, {"py": py + 1})

    def halo_copy(bufs, e, d, target):
        src, dst, ss, rs = bufs
        return pltpu.make_async_remote_copy(
            src_ref=src.at[e],
            dst_ref=dst.at[e, d],
            send_sem=ss.at[e, d],
            recv_sem=rs.at[e, d],
            device_id=place[target],
            device_id_type=MESH,
        )

    def halo_start(bufs, e, dirs):
        for d in reversed(range(dirs)):

            @pl.when(has[d ^ 1])
            def _(d=d):
                halo_copy(bufs, e, d, d ^ 1).start()

    def halo_recv(bufs, e, dirs):
        for d in range(dirs):

            @pl.when(has[d])
            def _(d=d):
                halo_copy(bufs, e, d, d).wait_recv()

    def halo_sent(bufs, uses, dirs):
        for e in uses:
            for d in range(dirs):

                @pl.when(has[d ^ 1])
                def _(d=d, e=e):
                    halo_copy(bufs, e, d, d ^ 1).wait_send()

    def sum_copy(axis, j):
        me, n, src, dst, ss, rs = (
            (px, npx, sum_x_src, sum_x, ss_x, rs_x)
            if axis == "px"
            else (py, npy, sum_y_src, sum_y, ss_y, rs_y)
        )
        return pltpu.make_async_remote_copy(
            src_ref=src,
            dst_ref=dst.at[j - 1],
            send_sem=ss.at[j - 1],
            recv_sem=rs.at[j - 1],
            device_id={axis: lax.rem(me + j, n)},
            device_id_type=MESH,
        )

    def all_sum(axis, n, src, dst, value):
        src[...] = value
        for j in range(1, n):
            sum_copy(axis, j).start()
        for j in range(1, n):
            sum_copy(axis, j).wait_recv()
        total = value
        for j in range(1, n):
            total = total + dst[j - 1]
        return total

    def split_cols(stage, w, b):
        high, low = halves(stage[b])
        w[b, :, :node] = high.astype(BF16)
        w[b, :, node:] = low.astype(BF16)

    def split_rows(stage, w, b):
        high, low = halves(stage[b])
        w[b, :node, :] = high.astype(BF16)
        w[b, node:, :] = low.astype(BF16)

    def split_all(i, stage, w, how):
        whole_copy(i).wait()

        @pl.loop(0, stage.shape[0])
        def _(b):
            how(stage, w, b)

    def split_couple_fine():
        for i in range(parts):
            couple_copy(i).wait()

            @pl.loop(i * per_part, (i + 1) * per_part)
            def _(b):
                split_cols(stage_cf, w_cf, b)

    def split_inverse():
        whole_copy(8).wait()
        size = inverse.shape[0]

        @pl.loop(0, size // node)
        def _(b):
            rows = pl.ds(pl.multiple_of(b * node, node), node)
            high, low = halves(stage_inv[rows, :])
            w_inv[rows, :size] = high.astype(BF16)
            w_inv[rows, size:] = low.astype(BF16)

    def apply(v, e, level, before_diag=None, before_couple=None, sent=False, following=None):
        count, vec, ext, acc, bufs, dirs, links, send, w_d, w_c = level
        shared = send.shape[1]
        if not sent:
            vec[:count] = v
            for h in range(shared):
                bufs[0][e, h] = vec[send[0, h]]
            halo_start(bufs, e, dirs)
        ext[:count] = rows_split(v)
        if before_diag is not None:
            before_diag()

        def own(b, carry):
            acc[b] = quarters(jnp.dot(ext[b], w_d[b], preferred_element_type=F32))
            return carry

        lax.fori_loop(0, count, own, 0, unroll=True)
        if before_couple is not None:
            before_couple()
        halo_recv(bufs, e, dirs)
        for d in range(dirs):
            ext[count + d * shared : count + (d + 1) * shared] = rows_split(bufs[1][e, d])

        def product(b):
            picked = jnp.concatenate([ext[links(b, k)] for k in range(width_k)], axis=1)
            return acc[b] + quarters(jnp.dot(picked, w_c[b], preferred_element_type=F32))

        if following is not None:
            p, q, keep = following
            vec[:count] = p
            for h in range(shared):
                b = send[0, h]
                z = product(b)
                if keep is not None:
                    z = z * keep(b)
                bufs[0][e + 1, h] = vec[b] - q[0] * z
            halo_start(bufs, e + 1, dirs)

        def far(b, carry):
            acc[b] = product(b)
            return carry

        lax.fori_loop(0, count, far, 0, unroll=True)
        return acc[:count]

    def restrict(r, w_p, owner, count, groups, split):
        split[:count] = rows_split(r)
        totals = [jnp.zeros(r.shape[1:], F32) for _ in range(groups)]
        for b in range(count):
            piece = quarters(
                lax.dot_general(
                    split[b], w_p[b], (((1,), (1,)), ((), ())), preferred_element_type=F32
                )
            )
            for c in range(groups):
                totals[c] = totals[c] + piece * jnp.where(owner[0, b] == c, 1.0, 0.0)
        return jnp.stack(totals)

    def prolong(u, w_p, owner, count, split):
        split[: u.shape[0]] = rows_split(u)
        out = []
        for b in range(count):
            part = split[owner[0, b]]
            z = jnp.dot(
                jnp.concatenate([part, part], axis=1), w_p[b], preferred_element_type=F32
            )
            out.append(z[: z.shape[0] // 2] + z[z.shape[0] // 2 :])
        return jnp.stack(out)

    def terms(level):
        shape = out.shape[2:]
        low = jnp.full(shape, cheb_low[level], F32)
        high = jnp.full(shape, cheb_high[level], F32)
        center = 0.5 * (high + low)
        half_width = 0.5 * (high - low)
        ratio = center / half_width
        first = 1.0 / ratio
        second = 1.0 / (2.0 * ratio - first)
        return (1.0 / center)[None], (second * first)[None], (2.0 * second / half_width)[None]

    bufs_f = (sbuf_f, rbuf_f, ss_f, rs_f)
    bufs_m = (sbuf_m, rbuf_m, ss_m, rs_m)
    bufs_r = (sbuf_r, rbuf_r, ss_r, rs_r)
    level_f = (fine, vec_f, ext_f, acc_f, bufs_f, 4, lambda b, k: links_fine[k, b], send_fine, w_df, w_cf)
    level_m = (mid, vec_c, ext_c, acc_c, bufs_m, 4, lambda b, k: links_mid[b, k], send_mid, w_dm, w_cm)
    level_r = (row, vec_c, ext_c, acc_c, bufs_r, 2, lambda b, k: links_row[b, k], send_row, w_dr, w_cr)

    for copy in small:
        copy.wait()
    mask = jnp.where(
        lax.broadcasted_iota(jnp.int32, right_side.shape, 0) < live[0, 0], 1.0, 0.0
    ).astype(F32)

    def is_live(b):
        return jnp.where(b < live[0, 0], 1.0, 0.0)

    inv_c, carry_c, gain_c = terms(0)
    target = right_side[...] * mask
    b_f[...] = target
    d = target * inv_c
    pl.semaphore_wait(barrier, npx + npy - 2)
    ad = apply(
        d,
        0,
        level_f,
        before_diag=lambda: split_all(0, stage_df, w_df, split_cols),
        before_couple=split_couple_fine,
        following=(carry_c * d + gain_c * target, gain_c, is_live),
    )
    r = target - ad * mask
    d2 = carry_c * d + gain_c * r
    x_f[...] = d + d2

    def more():
        split_all(1, stage_pf, w_pf, split_rows)
        split_all(2, stage_dm, w_dm, split_cols)
        split_all(3, stage_cm, w_cm, split_cols)

    r = r - apply(d2, 1, level_f, before_couple=more, sent=True) * mask

    inv_c, carry_c, gain_c = terms(1)
    target = restrict(r, w_pf, owner_fine, fine, mid, split_f)
    b_m[...] = target
    d = target * inv_c
    r = target - apply(
        d,
        0,
        level_m,
        before_couple=lambda: split_all(4, stage_pm, w_pm, split_rows),
        following=(carry_c * d + gain_c * target, gain_c, None),
    )
    d2 = carry_c * d + gain_c * r
    x_m[...] = d + d2

    def row_split():
        split_all(5, stage_dr, w_dr, split_cols)
        split_all(6, stage_cr, w_cr, split_cols)
        split_all(7, stage_pr, w_pr, split_rows)

    r = r - apply(d2, 1, level_m, before_couple=row_split, sent=True)

    inv_c, carry_c, gain_c = terms(2)
    share = restrict(r, w_pm, owner_mid, mid, row, split_c)
    target = all_sum("py", npy, sum_y_src, sum_y, share)
    b_r[...] = target
    d = target * inv_c
    r = target - apply(
        d,
        0,
        level_r,
        before_couple=split_inverse,
        following=(carry_c * d + gain_c * target, gain_c, None),
    )
    d2 = carry_c * d + gain_c * r
    x_r[...] = d + d2
    r = r - apply(d2, 1, level_r, sent=True)

    part = restrict(r, w_pr, owner_row, row, top, split_c)
    top_target = all_sum("px", npx, sum_x_src, sum_x, part)
    flat = jnp.concatenate([rows_split(top_target[c]) for c in range(top)], axis=1)
    solved = quarters(jnp.dot(flat, w_inv[...], preferred_element_type=F32))
    top_sol = jnp.stack([solved[:, c * node : (c + 1) * node] for c in range(top)])

    x = x_r[...] + prolong(top_sol, w_pr, owner_row, row, split_c)
    x_r[...] = x
    r = b_r[...] - apply(x, 2, level_r, following=(inv_c * b_r[...], inv_c, None))
    d = r * inv_c
    x_r[...] += d
    r = r - apply(d, 3, level_r, sent=True)
    x = x_r[...] + carry_c * d + gain_c * r

    inv_c, carry_c, gain_c = terms(1)
    x = x_m[...] + prolong(x, w_pm, owner_mid, mid, split_c)
    x_m[...] = x
    r = b_m[...] - apply(x, 2, level_m, following=(inv_c * b_m[...], inv_c, None))
    d = r * inv_c
    x_m[...] += d
    r = r - apply(d, 3, level_m, sent=True)
    x = x_m[...] + carry_c * d + gain_c * r

    def coarse_sent():
        halo_sent(bufs_m, range(4), 4)
        halo_sent(bufs_r, range(4), 2)
        for j in range(1, npy):
            sum_copy("py", j).wait_send()
        for j in range(1, npx):
            sum_copy("px", j).wait_send()

    inv_c, carry_c, gain_c = terms(0)
    x = x_f[...] + prolong(x, w_pf, owner_fine, fine, split_c) * mask
    x_f[...] = x
    r = b_f[...] - apply(
        x, 2, level_f, before_couple=coarse_sent, following=(inv_c * b_f[...], inv_c, is_live)
    ) * mask
    d = r * inv_c
    x_f[...] += d
    r = (
        r
        - apply(
            d,
            3,
            level_f,
            before_couple=lambda: halo_sent(bufs_f, range(3), 4),
            sent=True,
            following=(carry_c * d + gain_c * r, gain_c, is_live),
        )
        * mask
    )
    d2 = carry_c * d + gain_c * r
    out[0] = x_f[...] + d2
    out[1] = r - apply(d2, 4, level_f, sent=True) * mask

    halo_sent(bufs_f, (3, 4), 4)


def body(
    right_side,
    live_blocks,
    diag_fine,
    couple_fine,
    links_fine,
    send_fine,
    prolong_fine,
    owner_fine,
    diag_mid,
    couple_mid,
    links_mid,
    send_mid,
    prolong_mid,
    owner_mid,
    diag_row,
    couple_row,
    links_row,
    send_row,
    prolong_row,
    owner_row,
    coarse_inverse,
    cheb_low,
    cheb_high,
):
    npx, npy = lax.axis_size("px"), lax.axis_size("py")
    fine, sides, node = right_side.shape[2:]
    mid = diag_mid.shape[2]
    row = diag_row.shape[1]
    k = couple_fine.shape[3]
    size = coarse_inverse.shape[0]
    top = size // node
    h0, h1, h2 = send_fine.shape[-1], send_mid.shape[-1], send_row.shape[-1]
    coarse_most = max(mid, row, top)
    ext_most = max(mid + 4 * h1, row + 2 * h2)

    scalars = (
        live_blocks,
        jnp.swapaxes(links_fine.reshape(fine, k), 0, 1),
        send_fine.reshape(1, h0),
        owner_fine.reshape(1, fine),
        links_mid.reshape(mid, k),
        send_mid.reshape(1, h1),
        owner_mid.reshape(1, mid),
        links_row.reshape(row, k),
        send_row,
        owner_row,
        cheb_low,
        cheb_high,
    )
    arrays = (
        diag_fine.reshape(fine, node, node),
        couple_fine.reshape(fine, k * node, node),
        prolong_fine.reshape(fine, node, node),
        diag_mid.reshape(mid, node, node),
        couple_mid.reshape(mid, k * node, node),
        prolong_mid.reshape(mid, node, node),
        diag_row.reshape(row, node, node),
        couple_row.reshape(row, k * node, node),
        prolong_row.reshape(row, node, node),
        coarse_inverse,
    )
    vm = pltpu.VMEM
    dma = pltpu.SemaphoreType.DMA
    scratch = [vm(a.shape, F32) for a in arrays]
    for count in (fine, mid, row):
        scratch += [
            vm((count, node, 2 * node), BF16),
            vm((count, k * node, 2 * node), BF16),
            vm((count, 2 * node, node), BF16),
        ]
    scratch.append(vm((size, 2 * size), BF16))
    scratch += [
        vm((fine, sides, node), F32),
        vm((fine + 4 * h0, 2 * sides, node), BF16),
        vm((fine, sides, node), F32),
        vm((coarse_most, sides, node), F32),
        vm((ext_most, 2 * sides, node), BF16),
        vm((coarse_most, sides, node), F32),
        vm((fine, 2 * sides, node), BF16),
        vm((coarse_most, 2 * sides, node), BF16),
    ]
    for count in (fine, mid, row):
        scratch += [vm((count, sides, node), F32)] * 2
    for uses, dirs, shared in ((5, 4, h0), (4, 4, h1), (4, 2, h2)):
        scratch += [
            vm((uses, shared, sides, node), F32),
            vm((uses, dirs, shared, sides, node), F32),
        ]
    scratch += [
        vm((row, sides, node), F32),
        vm((npy - 1, row, sides, node), F32),
        vm((top, sides, node), F32),
        vm((npx - 1, top, sides, node), F32),
        dma((4 if fine % 4 == 0 else 1,)),
        dma((9,)),
    ]
    for uses, dirs in ((5, 4), (4, 4), (4, 2)):
        scratch += [dma((uses, dirs))] * 2
    scratch += [dma((npy - 1,))] * 2 + [dma((npx - 1,))] * 2
    scratch.append(vm((fine, sides, node), F32))
    scratch += [pltpu.SMEM(a.shape, a.dtype) for a in scalars]
    scratch.append(dma((len(scalars) + 1,)))

    shape = jax.ShapeDtypeStruct((2, fine, sides, node), F32)
    products = fine * (k + 1) * 5 + (mid + row) * (k + 1) * 4 + 2 * (fine + mid + row) + 16
    out = pl.pallas_call(
        functools.partial(kernel, npx, npy),
        out_shape=shape,
        in_specs=[pl.BlockSpec(memory_space=pltpu.HBM)] * (len(scalars) + 1 + len(arrays)),
        out_specs=pl.BlockSpec(memory_space=pltpu.VMEM),
        scratch_shapes=scratch,
        compiler_params=pltpu.CompilerParams(
            collective_id=0, has_side_effects=True, vmem_limit_bytes=56 * 1024 * 1024
        ),
        cost_estimate=pl.CostEstimate(
            flops=products * 2 * sides * node * node * 4,
            bytes_accessed=sum(4 * a.size for a in arrays),
            transcendentals=0,
        ),
        name="vcycle",
    )(*scalars, right_side.reshape(fine, sides, node), *arrays)
    full = (1, 1, fine, sides, node)
    return out[0].reshape(full), out[1].reshape(full)


def solution(mesh):
    grid = P("px", "py")
    line = P("px")
    whole = P()
    return jax.shard_map(
        body,
        mesh=mesh,
        in_specs=(grid,) * 14 + (line,) * 6 + (whole,) * 3,
        out_specs=(grid, grid),
        check_vma=False,
    )
```
